256 devices in a mesh: dp: 32 (over z, x), fsdp: 8 (over y, core).
Axes of the slice: x: 4, y: 4, z: 8, core: 2. Of those that a mesh axis runs over, the one named last changes fastest.
Arguments:
- tokens: bfloat16 [4096, 8192], P('dp', 'fsdp'), may hold values from -170 to 170
- out_grad: bfloat16 [4096, 28672], P('dp'), may hold values from -0.25 to 0.25
- sketch_matrix: bfloat16 [4096, 256], P('dp'), may hold values from -4 to 4
- memory: bfloat16 [8192, 1024], P('fsdp'), may hold values from -1.5 to 1.5, as said below
Outputs:
- projected: bfloat16 [8192, 28672], P('fsdp', 'dp')
- new_basis: bfloat16 [8192, 256], P('fsdp')
The draws below stay inside these ranges and needn't reach their ends.
Inputs may be any that keep to these rules, and one draw needn't show every extreme that they name: memory's columns are orthonormal up to the bfloat16 rounding, scaled by sqrt(8192).
All inputs are finite; a program needn't handle non-finite values.
Results may differ from the reference program's by a relative error of at most 0.0062.
Values may be sent and summed in bfloat16 or wider, within the bound.
No kernel may reach another device: no remote copies, remote signals or barrier semaphores. Data moves between devices by JAX's collectives and lax.ppermute only.
A program may use at most 128 MiB of HBM per device.

```python
import math
import jax
import jax.numpy as jnp
from jax import lax

D = 8192
F = 28672
K = 1024
R = 256
TOKENS = 4096


def draw_tokens(key, part):
    key = jax.random.fold_in(key, 11)
    key_noise, key_rows, key_cols = jax.random.split(key, 3)
    row_place = jnp.arange(TOKENS, dtype=jnp.float32) / TOKENS
    col_place = jnp.arange(D, dtype=jnp.float32) / D
    row_scale = jnp.exp(jax.random.uniform(key_rows, (TOKENS,), jnp.float32, math.log(0.5), math.log(1.5))) * (1.0 + 2.0 * row_place)
    col_scale = jnp.exp(jax.random.uniform(key_cols, (D,), jnp.float32, math.log(0.3), math.log(3.0))) * (1.0 + 2.0 * col_place)
    base = jnp.clip(jax.random.normal(key_noise, (TOKENS, D), jnp.float32), -4.0, 4.0)
    return (base * row_scale[:, None] * col_scale[None, :]).astype(jnp.bfloat16)


def draw_sketch_matrix(key, part):
    key = jax.random.fold_in(key, 23)
    key_noise, key_cols = jax.random.split(key, 2)
    col_scale = jnp.exp(jax.random.uniform(key_cols, (R,), jnp.float32, math.log(0.1), math.log(1.0)))
    base = jnp.clip(jax.random.normal(key_noise, (TOKENS, R), jnp.float32), -4.0, 4.0)
    return (base * col_scale[None, :]).astype(jnp.bfloat16)


def draw_memory(key, part):
    key = jax.random.fold_in(key, 37)
    key_perm, key_signs, key_angles = jax.random.split(key, 3)
    chosen = jax.random.permutation(key_perm, D)[:K].astype(jnp.int32)
    row_ids = jnp.arange(D, dtype=jnp.int32)
    parity = jnp.zeros((D, K), jnp.int32)
    for level in range(D.bit_length()):
        row_bit = jnp.bitwise_and(jnp.right_shift(row_ids, level), 1)
        col_bit = jnp.bitwise_and(jnp.right_shift(chosen, level), 1)
        parity = parity + row_bit[:, None] * col_bit[None, :]
    hadamard = 1.0 - 2.0 * jnp.bitwise_and(parity, 1).astype(jnp.float32)
    signs = 1.0 - 2.0 * jax.random.randint(key_signs, (D,), 0, 2).astype(jnp.float32)
    signed = hadamard * signs[:, None]
    half = D // 2
    angles = jax.random.uniform(key_angles, (half,), jnp.float32, -math.pi, math.pi)
    cosine = jnp.cos(angles)[:, None]
    sine = jnp.sin(angles)[:, None]
    upper = signed[:half]
    lower = signed[half:]
    return jnp.concatenate([cosine * upper - sine * lower, sine * upper + cosine * lower], axis=0).astype(jnp.bfloat16)


def shard_levels(stream_key, dims, pieces, smallest, top_value):
    factor_of, own = 1.0, jax.random.fold_in(stream_key, 6)
    for dim, parts in pieces:
        draws = jnp.exp(jax.random.uniform(jax.random.fold_in(own, dim), (parts,), jnp.float32, smallest / len(pieces), top_value / len(pieces)))
        factor_of = factor_of * jnp.repeat(draws, dims[dim] // parts).reshape([-1 if axis == dim else 1 for axis in range(len(dims))])
    return factor_of


def normal_values(own_key, shape, scale, most, cuts=(), kind=jnp.bfloat16):
    array = jax.random.normal(own_key, shape, jnp.float32) * scale
    if len(cuts) > 0:
        array = shard_levels(own_key, shape, cuts, -0.22, 0.18) * array
    return jnp.clip(array, min=-most, max=most).astype(kind)


def setup_inputs(seed: int = 0) -> dict:
    key_list = jax.random.split(jax.random.key(seed), 5)
    tokens = draw_tokens(jax.random.fold_in(key_list[4], 71), 0)
    out_grad = normal_values(key_list[1], (TOKENS, F), (TOKENS ** -0.5), 0.25, ((0, 32),))
    sketch_matrix = draw_sketch_matrix(jax.random.fold_in(key_list[4], 71), 0)
    memory = draw_memory(jax.random.fold_in(key_list[4], 71), 0)
    return {"tokens": tokens, "out_grad": out_grad, "sketch_matrix": sketch_matrix, "memory": memory}


def reference(tokens, out_grad, sketch_matrix, memory):
    sketch = jnp.dot(tokens.T.astype(jnp.float32), sketch_matrix.astype(jnp.float32), preferred_element_type=jnp.float32).astype(jnp.bfloat16)
    sketch = lax.optimization_barrier(sketch)
    coef_first = jnp.dot(memory.T.astype(jnp.float32), sketch.astype(jnp.float32), preferred_element_type=jnp.float32)
    scaled_first = (coef_first / D).astype(jnp.bfloat16)
    first = sketch.astype(jnp.float32) - jnp.dot(memory.astype(jnp.float32), scaled_first.astype(jnp.float32), preferred_element_type=jnp.float32)
    gram = jnp.dot(first.T, first, precision=lax.Precision.HIGHEST)
    factor = jnp.linalg.cholesky(gram)
    basis = lax.linalg.triangular_solve(factor, first, left_side=False, lower=True, transpose_a=True)
    new_basis = (math.sqrt(D) * basis).astype(jnp.bfloat16)
    stacked = jnp.moveaxis(out_grad.reshape(out_grad.shape[0], 8, out_grad.shape[1] // 8), 1, 0)

    def project(columns):
        grad_round = jnp.dot(tokens.T.astype(jnp.float32), columns.astype(jnp.float32), preferred_element_type=jnp.float32).astype(jnp.bfloat16)
        grad_round = lax.optimization_barrier(grad_round)
        grad_wide = grad_round.astype(jnp.float32)
        coef_memory = jnp.dot(memory.T.astype(jnp.float32), grad_round.astype(jnp.float32), preferred_element_type=jnp.float32)
        scaled_memory = (coef_memory / D).astype(jnp.bfloat16)
        coef_basis = jnp.dot(basis.T, grad_wide, precision=lax.Precision.HIGHEST)
        correction = jnp.dot(memory.astype(jnp.float32), scaled_memory.astype(jnp.float32), preferred_element_type=jnp.float32)
        correction = correction + jnp.dot(basis, coef_basis, precision=lax.Precision.HIGHEST)
        return (grad_wide - correction).astype(jnp.bfloat16)
    results = lax.map(project, stacked)
    projected = jnp.moveaxis(results, 0, 1).reshape(memory.shape[0], out_grad.shape[1])
    return (projected, new_basis)
```

```python
import math

import jax
import jax.numpy as jnp
from jax import lax
from jax.sharding import PartitionSpec as P

D = 8192
DP, FS = 32, 8
BF, F32 = jnp.bfloat16, jnp.float32
HIGH = lax.Precision.HIGHEST


def contract_rows(left, right, precision=None):
    return lax.dot_general(
        left, right, (((0,), (0,)), ((), ())), precision=precision, preferred_element_type=F32
    )


def swap(x, axis):
    return lax.all_to_all(x, axis, split_axis=0, concat_axis=0, tiled=True)


def sum_scatter(x, axis, n):
    rows = x.shape[0] // n
    return jnp.sum(swap(x, axis).reshape(n, rows, x.shape[1]), axis=0)


def spread(x, axis, n):
    wide = jnp.broadcast_to(x[None], (n,) + x.shape).reshape(n * x.shape[0], x.shape[1])
    return swap(lax.optimization_barrier(wide), axis)


def local(tokens, out_grad, sketch_matrix, memory):
    f = lax.axis_index("fsdp")
    cols = out_grad.shape[1] // DP
    rows = tokens.shape[0] // FS
    token_part = jnp.dot(tokens, memory, preferred_element_type=F32)
    token_own = sum_scatter(token_part, "fsdp", FS)
    token_own = (token_own / D).astype(BF)
    token_coef = spread(token_own, "fsdp", FS)
    clean = tokens.astype(F32) - lax.dot_general(
        token_coef, memory, (((1,), (1,)), ((), ())), preferred_element_type=F32
    )
    clean = clean.astype(BF)
    clean_all = lax.all_gather(clean, "dp", axis=0, tiled=True)
    own = lax.dynamic_slice_in_dim(out_grad, f * rows, rows, 0)
    own = jnp.transpose(own.reshape(rows, DP, cols), (1, 0, 2))
    sk = lax.dynamic_slice_in_dim(sketch_matrix, f * rows, rows, 0)
    own = jnp.concatenate([own, jnp.broadcast_to(sk[None], (DP,) + sk.shape)], axis=2)
    part = swap(own, "dp")
    right = lax.all_gather(part, "fsdp", axis=0, tiled=False)
    right = jnp.transpose(right, (1, 0, 2, 3)).reshape(DP * FS * rows, -1)
    mine = lax.dynamic_slice_in_dim(token_coef, f * 128, 128, 1)
    coef = contract_rows(mine, sketch_matrix)
    coef = jnp.pad(coef.reshape(DP, 4, -1), ((0, 0), (0, 4), (0, 0))).reshape(DP * 8, -1)
    coef = sum_scatter(coef, "dp", DP)
    coef = spread(coef, "dp", DP).reshape(DP, 8, -1)[:, :4].reshape(DP * 4, -1)
    coef = lax.all_gather(coef, "fsdp", axis=0, tiled=True)
    both = contract_rows(clean_all, right)
    gradient, first = both[:, :cols], both[:, cols:]
    gram = contract_rows(first, first, HIGH)
    gram = spread(sum_scatter(gram, "fsdp", FS), "fsdp", FS)
    sketch = first + jnp.dot(memory, coef.astype(BF), preferred_element_type=F32)
    weight = contract_rows(sketch, gradient, HIGH)
    weight = spread(sum_scatter(weight, "fsdp", FS), "fsdp", FS)
    factor = jnp.linalg.cholesky(gram)
    inverse = lax.linalg.triangular_solve(
        factor, jnp.eye(factor.shape[0], dtype=F32), left_side=True, lower=True
    )
    basis = lax.dot_general(first, inverse, (((1,), (1,)), ((), ())), precision=HIGH)
    coef_basis = jnp.dot(inverse, weight, precision=HIGH)
    projected = (gradient - jnp.dot(basis, coef_basis, precision=HIGH)).astype(BF)
    new_basis = (math.sqrt(D) * basis).astype(BF)
    return (projected, new_basis)


def solution(mesh):
    in_specs = (P("dp", "fsdp"), P("dp", None), P("dp", None), P("fsdp", None))
    out_specs = (P("fsdp", "dp"), P("fsdp", None))
    return jax.shard_map(local, mesh=mesh, in_specs=in_specs, out_specs=out_specs, check_vma=False)
```

```python
import functools
import math

import jax
import jax.numpy as jnp
from jax import lax
from jax.experimental import pallas as pl
from jax.experimental.pallas import tpu as pltpu
from jax.sharding import PartitionSpec as P

D = 8192
DP, FS, NZ, NX, NY = 32, 8, 8, 4, 4
BF, F32 = jnp.bfloat16, jnp.float32
HIGH = lax.Precision.HIGHEST
PANEL = 64


def inverse_factor_kernel(a_ref, x_ref, w_ref):
    n = a_ref.shape[0]
    w_ref[...] = a_ref[...]
    lane = lax.broadcasted_iota(jnp.int32, (PANEL, n), 1)
    sub = lax.broadcasted_iota(jnp.int32, (PANEL, n), 0)
    for r0 in range(0, n, PANEL):
        p = w_ref[r0 : r0 + PANEL, :]
        for j in range(PANEL):
            c = r0 + j
            scale = lax.rsqrt(p[j : j + 1, c : c + 1])
            row = jnp.where(lane[:1] == c, 1.0, p[j : j + 1, :]) * scale
            column = p[:, c : c + 1] * scale
            new = jnp.where(lane == c, 0.0, p) - column * row
            p = jnp.where(sub > j, new, p)
            p = jnp.where(sub == j, row, p)
        done = jnp.where(lane <= sub + r0, p, 0.0)
        x_ref[r0 : r0 + PANEL, :] = done
        r1 = r0 + PANEL
        if r1 < n:
            wide = jnp.where(lane < r1, done, p)
            step = jnp.dot(p.T[r1:, :], wide, precision=HIGH, preferred_element_type=F32)
            rest = w_ref[r1:, :]
            at = lax.broadcasted_iota(jnp.int32, rest.shape, 1)
            w_ref[r1:, :] = jnp.where((at >= r0) & (at < r1), 0.0, rest) - step


def inverse_factor(gram):
    n = gram.shape[0]
    return pl.pallas_call(
        inverse_factor_kernel,
        out_shape=jax.ShapeDtypeStruct((n, n), F32),
        scratch_shapes=[pltpu.VMEM((n, n), F32)],
        cost_estimate=pl.CostEstimate(flops=60_000_000_000, bytes_accessed=1 << 20, transcendentals=256),
        name="inverse_factor",
    )(gram)


def contract_rows(left, right, precision=None):
    return lax.dot_general(
        left, right, (((0,), (0,)), ((), ())), precision=precision, preferred_element_type=F32
    )


def swap(x, axis):
    return lax.all_to_all(x, axis, split_axis=0, concat_axis=0, tiled=True)


def sum_scatter(x, axis, n):
    rows = x.shape[0] // n
    return jnp.sum(swap(x, axis).reshape(n, rows, x.shape[1]), axis=0)


def spread(x, axis, n):
    wide = jnp.broadcast_to(x[None], (n,) + x.shape).reshape(n * x.shape[0], x.shape[1])
    return swap(lax.optimization_barrier(wide), axis)


def shift_dp(x, dz, dx):
    pairs = [
        (z * NX + c, ((z + dz) % NZ) * NX + (c + dx) % NX) for z in range(NZ) for c in range(NX)
    ]
    return lax.ppermute(x, "dp", pairs)


def shift_fs(x, dy, dc):
    pairs = [(y * 2 + c, ((y + dy) % NY) * 2 + (c + dc) % 2) for y in range(NY) for c in range(2)]
    return lax.ppermute(x, "fsdp", pairs)


def block(x, i, rows):
    return lax.dynamic_slice_in_dim(x, i * rows, rows, 0)


def fs_scatter(x):
    f = lax.axis_index("fsdp")
    y, c = f // 2, f % 2
    half, rows = x.shape[0] // 2, x.shape[0] // 8
    mine = block(x, c, half) + shift_fs(block(x, 1 - c, half), 0, 1)
    parts = [block(mine, y, rows)]
    for dy in (1, 3, 2):
        parts.append(shift_fs(block(mine, (y + dy) % NY, rows), dy, 0))
    return (parts[0] + parts[1]) + (parts[2] + parts[3])


def fs_gather(x):
    f = lax.axis_index("fsdp")
    y, c = f // 2, f % 2
    rows = x.shape[0]
    half = jnp.zeros((4 * rows, x.shape[1]), x.dtype)
    half = lax.dynamic_update_slice(half, x, (y * rows, 0))
    for dy in (1, 3, 2):
        half = lax.dynamic_update_slice(half, shift_fs(x, dy, 0), (((y - dy) % NY) * rows, 0))
    other = shift_fs(half, 0, 1)
    first = jnp.where(c == 0, half, other)
    second = jnp.where(c == 0, other, half)
    return jnp.concatenate([first, second], axis=0)


def gather_tokens(x):
    d = lax.axis_index("dp")
    z, c = d // NX, d % NX
    width = x.shape[1]
    rows = x.shape[0] // FS
    full = jnp.zeros((FS, NZ, NX, rows, width), x.dtype)

    def put(full, part, f0, dz, dx):
        part = part.reshape(-1, 1, 1, rows, width)
        return lax.dynamic_update_slice(full, part, (f0, (z - dz) % NZ, (c - dx) % NX, 0, 0))

    upper, lower = x[: 4 * rows], x[4 * rows :]
    streams = [upper] + [shift_dp(upper, 0, dx) for dx in (1, 2, 3)]
    ahead = [(lower, 0)]
    fw, bw = lower, lower
    for s in (1, 2, 3):
        fw, bw = shift_dp(fw, 1, 0), shift_dp(bw, -1, 0)
        ahead += [(fw, s), (bw, -s)]
    last = jnp.concatenate(
        [shift_dp(fw[: 2 * rows], 1, 0), shift_dp(bw[2 * rows :], -1, 0)], axis=0
    )
    ahead.append((last, 4))
    placed = []
    for dx in range(NX):
        fw = bw = streams[dx]
        placed.append((fw, 0, 0, dx))
        for s in (1, 2, 3):
            fw, bw = shift_dp(fw, 1, 0), shift_dp(bw, -1, 0)
            placed += [(fw, 0, s, dx), (bw, 0, -s, dx)]
        placed.append((shift_dp(fw, 1, 0) if dx < 2 else shift_dp(bw, -1, 0), 0, 4, dx))
    for part, s in ahead:
        right, left = shift_dp(part, 0, 1), shift_dp(part, 0, -1)
        placed += [(part, 4, s, 0), (right, 4, s, 1), (left, 4, s, -1)]
        placed.append((shift_dp(right[: 2 * rows], 0, 1), 4, s, 2))
        placed.append((shift_dp(left[2 * rows :], 0, -1), 6, s, 2))
    for part, f0, dz, dx in placed:
        full = put(full, part, f0, dz, dx)
    return full.reshape(DP * FS * rows, width)


def local(tokens, out_grad, sketch_matrix, memory):
    f = lax.axis_index("fsdp")
    cols = out_grad.shape[1] // DP
    rows = tokens.shape[0] // FS
    own = lax.dynamic_slice_in_dim(out_grad, f * rows, rows, 0)
    own = jnp.transpose(own.reshape(rows, DP, cols), (1, 0, 2))
    sk = lax.dynamic_slice_in_dim(sketch_matrix, f * rows, rows, 0)
    own = jnp.concatenate([own, jnp.broadcast_to(sk[None], (DP,) + sk.shape)], axis=2)
    part = swap(own, "dp")
    right = lax.all_gather(part, "fsdp", axis=0, tiled=False)
    right = right.reshape(DP * FS * rows, -1)
    token_part = jnp.dot(tokens, memory, preferred_element_type=F32)
    token_coef = fs_gather((fs_scatter(token_part) / D).astype(BF))
    clean = tokens.astype(F32) - lax.dot_general(
        token_coef, memory, (((1,), (1,)), ((), ())), preferred_element_type=F32
    )
    clean_all = gather_tokens(clean.astype(BF))
    mine = lax.dynamic_slice_in_dim(token_coef, f * 128, 128, 1)
    coef = contract_rows(mine, sketch_matrix)
    coef = jnp.pad(coef.reshape(DP, 4, -1), ((0, 0), (0, 4), (0, 0))).reshape(DP * 8, -1)
    coef = sum_scatter(coef, "dp", DP)
    coef = spread(coef, "dp", DP).reshape(DP, 8, -1)[:, :4].reshape(DP * 4, -1)
    coef = lax.all_gather(coef.astype(BF), "fsdp", axis=0, tiled=True)
    first = contract_rows(clean_all, right[:, cols:])
    gram = fs_gather(fs_scatter(contract_rows(first, first, HIGH)))
    gradient = contract_rows(clean_all, right[:, :cols])
    sketch = first + jnp.dot(memory, coef, preferred_element_type=F32)
    weight = fs_gather(fs_scatter(contract_rows(sketch, gradient, HIGH)))
    inverse = inverse_factor(gram)
    basis = lax.dot_general(first, inverse, (((1,), (1,)), ((), ())), precision=HIGH)
    coef_basis = jnp.dot(inverse, weight, precision=HIGH)
    projected = (gradient - jnp.dot(basis, coef_basis, precision=HIGH)).astype(BF)
    new_basis = (math.sqrt(D) * basis).astype(BF)
    return (projected, new_basis)


def solution(mesh):
    in_specs = (P("dp", "fsdp"), P("dp", None), P("dp", None), P("fsdp", None))
    out_specs = (P("fsdp", "dp"), P("fsdp", None))
    return jax.shard_map(local, mesh=mesh, in_specs=in_specs, out_specs=out_specs, check_vma=False)
```

```python
import math

import jax
import jax.numpy as jnp
from jax import lax
from jax.experimental import pallas as pl
from jax.experimental.pallas import tpu as pltpu
from jax.sharding import PartitionSpec as P

D = 8192
DP, FS, NY = 32, 8, 4
BF, F32 = jnp.bfloat16, jnp.float32
HIGH = lax.Precision.HIGHEST
PANEL = 64


def factor_panels(first_panel, last_panel, w_ref, x_ref):
    n = w_ref.shape[0]
    lane = lax.broadcasted_iota(jnp.int32, (PANEL, n), 1)
    sub = lax.broadcasted_iota(jnp.int32, (PANEL, n), 0)
    for r0 in range(first_panel * PANEL, last_panel * PANEL, PANEL):
        p = w_ref[r0 : r0 + PANEL, :]
        for j in range(PANEL):
            c = r0 + j
            scale = lax.rsqrt(p[j : j + 1, c : c + 1])
            row = jnp.where(lane[:1] == c, 1.0, p[j : j + 1, :]) * scale
            column = p[:, c : c + 1] * scale
            new = jnp.where(lane == c, 0.0, p) - column * row
            p = jnp.where(sub > j, new, p)
            p = jnp.where(sub == j, row, p)
        done = jnp.where(lane <= sub + r0, p, 0.0)
        x_ref[r0 : r0 + PANEL, :] = done
        r1 = r0 + PANEL
        if r1 < n:
            wide = jnp.where(lane < r1, done, p)
            step = jnp.dot(p.T[r1:, :], wide, precision=HIGH, preferred_element_type=F32)
            rest = w_ref[r1:, :]
            at = lax.broadcasted_iota(jnp.int32, rest.shape, 1)
            w_ref[r1:, :] = jnp.where((at >= r0) & (at < r1), 0.0, rest) - step


def factor_front(a_ref, x_ref, w_ref):
    w_ref[...] = a_ref[...]
    factor_panels(0, 2, w_ref, x_ref)
    x_ref[2 * PANEL :, :] = w_ref[2 * PANEL :, :]


def factor_back(a_ref, x_ref, w_ref):
    w_ref[...] = a_ref[...]
    x_ref[...] = a_ref[...]
    factor_panels(2, 4, w_ref, x_ref)


def factor_half(body, x, name):
    return pl.pallas_call(
        body,
        out_shape=jax.ShapeDtypeStruct(x.shape, F32),
        scratch_shapes=[pltpu.VMEM(x.shape, F32)],
        cost_estimate=pl.CostEstimate(flops=14_000_000_000, bytes_accessed=1 << 20, transcendentals=256),
        name=name,
    )(x)


def contract_rows(left, right, precision=None):
    return lax.dot_general(
        left, right, (((0,), (0,)), ((), ())), precision=precision, preferred_element_type=F32
    )


def swap(x, axis):
    return lax.all_to_all(x, axis, split_axis=0, concat_axis=0, tiled=True)


def sum_scatter(x, axis, n):
    rows = x.shape[0] // n
    return jnp.sum(swap(x, axis).reshape(n, rows, x.shape[1]), axis=0)


def spread(x, axis, n):
    wide = jnp.broadcast_to(x[None], (n,) + x.shape).reshape(n * x.shape[0], x.shape[1])
    return swap(lax.optimization_barrier(wide), axis)


def shift_fs(x, dy, dc):
    pairs = [(y * 2 + c, ((y + dy) % NY) * 2 + (c + dc) % 2) for y in range(NY) for c in range(2)]
    return lax.ppermute(x, "fsdp", pairs)


def block(x, i, rows):
    return lax.dynamic_slice_in_dim(x, i * rows, rows, 0)


def fs_scatter(x):
    f = lax.axis_index("fsdp")
    y, c = f // 2, f % 2
    half, rows = x.shape[0] // 2, x.shape[0] // 8
    mine = block(x, c, half) + shift_fs(block(x, 1 - c, half), 0, 1)
    parts = [block(mine, y, rows)]
    for dy in (1, 3, 2):
        parts.append(shift_fs(block(mine, (y + dy) % NY, rows), dy, 0))
    return (parts[0] + parts[1]) + (parts[2] + parts[3])


def fs_gather(x):
    f = lax.axis_index("fsdp")
    y, c = f // 2, f % 2
    rows = x.shape[0]
    half = jnp.zeros((4 * rows, x.shape[1]), x.dtype)
    half = lax.dynamic_update_slice(half, x, (y * rows, 0))
    for dy in (1, 3, 2):
        half = lax.dynamic_update_slice(half, shift_fs(x, dy, 0), (((y - dy) % NY) * rows, 0))
    other = shift_fs(half, 0, 1)
    first = jnp.where(c == 0, half, other)
    second = jnp.where(c == 0, other, half)
    return jnp.concatenate([first, second], axis=0)


def fs_sum(x):
    f = lax.axis_index("fsdp")
    y, c = f // 2, f % 2
    half = x.shape[0] // 2
    mine = block(x, c, half) + shift_fs(block(x, 1 - c, half), 0, 1)
    parts = jnp.zeros((4,) + mine.shape, x.dtype)
    parts = lax.dynamic_update_slice(parts, mine[None], (y, 0, 0))
    for dy in (1, 3, 2):
        parts = lax.dynamic_update_slice(parts, shift_fs(mine, dy, 0)[None], ((y - dy) % NY, 0, 0))
    mine = (parts[0] + parts[1]) + (parts[2] + parts[3])
    other = shift_fs(mine, 0, 1)
    return jnp.concatenate([jnp.where(c == 0, mine, other), jnp.where(c == 0, other, mine)], axis=0)


def local(tokens, out_grad, sketch_matrix, memory):
    f = lax.axis_index("fsdp")
    cols = out_grad.shape[1] // DP
    rows = tokens.shape[0] // FS
    own = lax.dynamic_slice_in_dim(out_grad, f * rows, rows, 0)
    own = jnp.transpose(own.reshape(rows, DP, cols), (1, 0, 2))
    sk = lax.dynamic_slice_in_dim(sketch_matrix, f * rows, rows, 0)
    own = jnp.concatenate([own, jnp.broadcast_to(sk[None], (DP,) + sk.shape)], axis=2)
    part = swap(own, "dp")
    token_part = jnp.dot(tokens, memory, preferred_element_type=F32)
    token_coef = fs_gather((fs_scatter(token_part) / D).astype(BF))
    clean = tokens.astype(F32) - lax.dot_general(
        token_coef, memory, (((1,), (1,)), ((), ())), preferred_element_type=F32
    )
    clean = clean.astype(BF)
    clean_all = lax.all_gather(clean, "dp", axis=0, tiled=True)
    part, clean, token_coef = lax.optimization_barrier((part, clean, token_coef))
    right = lax.all_gather(part, "fsdp", axis=0, tiled=False)
    right = jnp.transpose(right, (1, 0, 2, 3)).reshape(DP * FS * rows, -1)
    omega, right = lax.optimization_barrier((right[:, cols:], right[:, :cols]))
    mine = lax.dynamic_slice_in_dim(token_coef, f * 128, 128, 1)
    coef = contract_rows(mine, sketch_matrix)
    coef = jnp.pad(coef.reshape(DP, 4, -1), ((0, 0), (0, 4), (0, 0))).reshape(DP * 8, -1)
    coef = sum_scatter(coef, "dp", DP)
    coef = spread(coef, "dp", DP).reshape(DP, 8, -1)[:, :4].reshape(DP * 4, -1)
    coef = lax.all_gather(coef.astype(BF), "fsdp", axis=0, tiled=True)
    first = contract_rows(clean_all, omega)
    gram = fs_sum(contract_rows(first, first, HIGH))
    gradient = contract_rows(clean_all, right)
    sketch = first + jnp.dot(memory, coef, preferred_element_type=F32)
    weight = contract_rows(sketch, gradient, lax.Precision.HIGH)
    weight = sum_scatter(weight, "fsdp", FS)
    state = factor_half(factor_front, gram, "factor_front")
    weight = spread(weight, "fsdp", FS)
    inverse = factor_half(factor_back, state, "factor_back")
    basis = lax.dot_general(first, inverse, (((1,), (1,)), ((), ())), precision=HIGH)
    coef_basis = jnp.dot(inverse, weight, precision=HIGH)
    correction = jnp.dot(basis, coef_basis, precision=lax.Precision.HIGH)
    projected = (gradient - correction).astype(BF)
    new_basis = (math.sqrt(D) * basis).astype(BF)
    return (projected, new_basis)


def solution(mesh):
    in_specs = (P("dp", "fsdp"), P("dp", None), P("dp", None), P("fsdp", None))
    out_specs = (P("fsdp", "dp"), P("fsdp", None))
    return jax.shard_map(local, mesh=mesh, in_specs=in_specs, out_specs=out_specs, check_vma=False)
```

```python
import math

import jax
import jax.numpy as jnp
from jax import lax
from jax.experimental import pallas as pl
from jax.experimental.pallas import tpu as pltpu
from jax.sharding import PartitionSpec as P

D = 8192
DP, FS, NY = 32, 8, 4
BF, F32 = jnp.bfloat16, jnp.float32
HIGH = lax.Precision.HIGHEST
PANEL = 32


def factor_panels(first_panel, last_panel, w_ref, x_ref):
    n = w_ref.shape[0]
    lane = lax.broadcasted_iota(jnp.int32, (PANEL, n), 1)
    sub = lax.broadcasted_iota(jnp.int32, (PANEL, n), 0)
    for r0 in range(first_panel * PANEL, last_panel * PANEL, PANEL):
        p = w_ref[r0 : r0 + PANEL, :]
        scale = jnp.ones((PANEL, n), F32)
        for j in range(0, PANEL, 2):
            c = r0 + j
            left = jnp.broadcast_to(p[:, c : c + 1], (PANEL, n))
            next_left = jnp.broadcast_to(p[:, c + 1 : c + 2], (PANEL, n))
            pivot, mixed = left[j : j + 1, :], left[j + 1 : j + 2, :]
            ratio = mixed * (1.0 / pivot)
            next_pivot = next_left[j + 1 : j + 2, :] - ratio * mixed
            at, next_at = lane == c, lane == c + 1
            row = jnp.where(at[:1], 1.0, p[j : j + 1, :])
            scaled = row * (1.0 / pivot)
            next_row = jnp.where(at[:1], 0.0, p[j + 1 : j + 2, :]) - mixed * scaled
            next_row = jnp.where(next_at[:1], 1.0, next_row)
            next_scaled = next_row * (1.0 / next_pivot)
            scaled = jnp.where(next_at[:1], 0.0, scaled)
            below = sub > j + 1
            base = jnp.where((at | next_at) & below, 0.0, p)
            base = base - jnp.where(below, left, 0.0) * scaled
            base = base - jnp.where(below, next_left - left * ratio, 0.0) * next_scaled
            p = jnp.where(sub == j, row, jnp.where(sub == j + 1, next_row, base))
            scale = jnp.where(sub == j, pivot, jnp.where(sub == j + 1, next_pivot, scale))
        p = p * lax.rsqrt(scale)
        done = jnp.where(lane <= sub + r0, p, 0.0)
        x_ref[r0 : r0 + PANEL, :] = done
        r1 = r0 + PANEL
        if r1 < n:
            wide = jnp.where(lane < r1, done, p)
            step = jnp.dot(p.T[r1:, :], wide, precision=HIGH, preferred_element_type=F32)
            rest = w_ref[r1:, :]
            at = lax.broadcasted_iota(jnp.int32, rest.shape, 1)
            w_ref[r1:, :] = jnp.where((at >= r0) & (at < r1), 0.0, rest) - step


def factor_front(a_ref, x_ref, w_ref):
    w_ref[...] = a_ref[...]
    factor_panels(0, 4, w_ref, x_ref)
    x_ref[4 * PANEL :, :] = w_ref[4 * PANEL :, :]


def factor_back(a_ref, x_ref, w_ref):
    w_ref[...] = a_ref[...]
    x_ref[...] = a_ref[...]
    factor_panels(4, 8, w_ref, x_ref)


def factor_half(body, x, name):
    return pl.pallas_call(
        body,
        out_shape=jax.ShapeDtypeStruct(x.shape, F32),
        scratch_shapes=[pltpu.VMEM(x.shape, F32)],
        cost_estimate=pl.CostEstimate(flops=9_000_000_000, bytes_accessed=1 << 20, transcendentals=256),
        name=name,
    )(x)


def contract_rows(left, right, precision=None):
    return lax.dot_general(
        left, right, (((0,), (0,)), ((), ())), precision=precision, preferred_element_type=F32
    )


def swap(x, axis):
    return lax.all_to_all(x, axis, split_axis=0, concat_axis=0, tiled=True)


def sum_scatter(x, axis, n):
    rows = x.shape[0] // n
    return jnp.sum(swap(x, axis).reshape(n, rows, x.shape[1]), axis=0)


def spread(x, axis, n):
    wide = jnp.broadcast_to(x[None], (n,) + x.shape).reshape(n * x.shape[0], x.shape[1])
    return swap(lax.optimization_barrier(wide), axis)


def shift_fs(x, dy, dc):
    pairs = [(y * 2 + c, ((y + dy) % NY) * 2 + (c + dc) % 2) for y in range(NY) for c in range(2)]
    return lax.ppermute(x, "fsdp", pairs)


def block(x, i, rows):
    return lax.dynamic_slice_in_dim(x, i * rows, rows, 0)


def fs_sum(x, kind, scale=1.0, hold=None):
    c = lax.axis_index("fsdp") % 2
    half = x.shape[0] // 2
    mine = (block(x, c, half) + shift_fs(block(x, 1 - c, half), 0, 1)).astype(kind)
    if hold is not None:
        mine, hold = lax.optimization_barrier((mine, hold))
    near, back, far = [shift_fs(mine, dy, 0).astype(F32) for dy in (1, 3, 2)]
    mine = (((mine.astype(F32) + near) + (back + far)) * scale).astype(kind)
    other = shift_fs(mine, 0, 1)
    total = jnp.concatenate([jnp.where(c == 0, mine, other), jnp.where(c == 0, other, mine)], axis=0)
    return total if hold is None else (total, hold)


def y_gather(x, cols):
    f = lax.axis_index("fsdp")
    y, c = f // 2, f % 2
    near, back = shift_fs(x, 1, 0), shift_fs(x, 3, 0)
    half = x.shape[0] // 2
    far = jnp.concatenate([shift_fs(near[:half], 1, 0), shift_fs(back[half:], 3, 0)], axis=0)
    main = jnp.zeros((DP, FS, x.shape[1], cols), x.dtype)
    rest = jnp.zeros((DP, FS, x.shape[1], x.shape[2] - cols), x.dtype)
    for part, dy in ((x, 0), (near, 1), (back, 3), (far, 2)):
        for piece, core in ((part, c), (shift_fs(part, 0, 1), 1 - c)):
            at = (0, ((y - dy) % NY) * 2 + core, 0, 0)
            main = lax.dynamic_update_slice(main, piece[:, None, :, :cols], at)
            rest = lax.dynamic_update_slice(rest, piece[:, None, :, cols:], at)
    return main.reshape(-1, cols), rest.reshape(-1, rest.shape[3])


def local(tokens, out_grad, sketch_matrix, memory):
    f = lax.axis_index("fsdp")
    cols = out_grad.shape[1] // DP
    rows = tokens.shape[0] // FS
    own = lax.dynamic_slice_in_dim(out_grad, f * rows, rows, 0)
    own = jnp.transpose(own.reshape(rows, DP, cols), (1, 0, 2))
    sk = lax.dynamic_slice_in_dim(sketch_matrix, f * rows, rows, 0)
    own = jnp.concatenate([own, jnp.broadcast_to(sk[None], (DP,) + sk.shape)], axis=2)
    part = swap(own, "dp")
    token_part = jnp.dot(tokens, memory, preferred_element_type=F32)
    token_coef = fs_sum(token_part, BF, 1.0 / D)
    clean = tokens.astype(F32) - lax.dot_general(
        token_coef, memory, (((1,), (1,)), ((), ())), preferred_element_type=F32
    )
    clean = clean.astype(BF)
    clean_all = lax.all_gather(clean, "dp", axis=0, tiled=True)
    part, clean, token_coef = lax.optimization_barrier((part, clean, token_coef))
    right, omega = y_gather(part, cols)
    mine = lax.dynamic_slice_in_dim(token_coef, f * 128, 128, 1)
    coef = contract_rows(mine, sketch_matrix)
    coef = jnp.pad(coef.reshape(DP, 4, -1), ((0, 0), (0, 4), (0, 0))).reshape(DP * 8, -1)
    coef = sum_scatter(coef, "dp", DP)
    coef = spread(coef, "dp", DP).reshape(DP, 8, -1)[:, :4].reshape(DP * 4, -1)
    coef = lax.all_gather(coef.astype(BF), "fsdp", axis=0, tiled=True)
    first = contract_rows(clean_all, omega)
    gram, held = fs_sum(contract_rows(first, first, HIGH), F32, hold=clean_all)
    half = memory.shape[0] // 2
    upper = contract_rows(clean_all[:, :half], right)
    lower = contract_rows(held[:, half:], right)
    sketch = first + jnp.dot(memory, coef, preferred_element_type=F32)
    weight = contract_rows(sketch[:half], upper, lax.Precision.HIGH)
    weight = weight + contract_rows(sketch[half:], lower, lax.Precision.HIGH)
    weight = sum_scatter(weight, "fsdp", FS)
    state = factor_half(factor_front, gram, "factor_front")
    weight = spread(weight, "fsdp", FS)
    inverse = factor_half(factor_back, state, "factor_back")
    basis = lax.dot_general(first, inverse, (((1,), (1,)), ((), ())), precision=HIGH)
    coef_basis = jnp.dot(inverse, weight, precision=HIGH)
    parts = []
    for piece, side in ((upper, basis[:half]), (lower, basis[half:])):
        correction = jnp.dot(side, coef_basis, precision=lax.Precision.HIGH)
        parts.append((piece - correction).astype(BF))
    projected = jnp.concatenate(parts, axis=0)
    new_basis = (math.sqrt(D) * basis).astype(BF)
    return (projected, new_basis)


def solution(mesh):
    in_specs = (P("dp", "fsdp"), P("dp", None), P("dp", None), P("fsdp", None))
    out_specs = (P("fsdp", "dp"), P("fsdp", None))
    return jax.shard_map(local, mesh=mesh, in_specs=in_specs, out_specs=out_specs, check_vma=False)
```

```python
import functools
import math

import jax
import jax.numpy as jnp
from jax import lax
from jax.experimental import pallas as pl
from jax.experimental.pallas import tpu as pltpu
from jax.sharding import PartitionSpec as P

D = 8192
DP, FS, NZ, NX, NY = 32, 8, 8, 4, 4
BF, F32 = jnp.bfloat16, jnp.float32
HIGH = lax.Precision.HIGHEST
PANEL = 32


def factor_panels(first_panel, last_panel, w_ref, x_ref):
    n = w_ref.shape[0]
    lane = lax.broadcasted_iota(jnp.int32, (PANEL, n), 1)
    sub = lax.broadcasted_iota(jnp.int32, (PANEL, n), 0)
    for r0 in range(first_panel * PANEL, last_panel * PANEL, PANEL):
        p = w_ref[r0 : r0 + PANEL, :]
        scale = jnp.ones((PANEL, n), F32)
        for j in range(0, PANEL, 2):
            c = r0 + j
            left = jnp.broadcast_to(p[:, c : c + 1], (PANEL, n))
            next_left = jnp.broadcast_to(p[:, c + 1 : c + 2], (PANEL, n))
            pivot, mixed = left[j : j + 1, :], left[j + 1 : j + 2, :]
            ratio = mixed * (1.0 / pivot)
            next_pivot = next_left[j + 1 : j + 2, :] - ratio * mixed
            at, next_at = lane == c, lane == c + 1
            row = jnp.where(at[:1], 1.0, p[j : j + 1, :])
            scaled = row * (1.0 / pivot)
            next_row = jnp.where(at[:1], 0.0, p[j + 1 : j + 2, :]) - mixed * scaled
            next_row = jnp.where(next_at[:1], 1.0, next_row)
            next_scaled = next_row * (1.0 / next_pivot)
            scaled = jnp.where(next_at[:1], 0.0, scaled)
            below = sub > j + 1
            base = jnp.where((at | next_at) & below, 0.0, p)
            base = base - jnp.where(below, left, 0.0) * scaled
            base = base - jnp.where(below, next_left - left * ratio, 0.0) * next_scaled
            p = jnp.where(sub == j, row, jnp.where(sub == j + 1, next_row, base))
            scale = jnp.where(sub == j, pivot, jnp.where(sub == j + 1, next_pivot, scale))
        p = p * lax.rsqrt(scale)
        done = jnp.where(lane <= sub + r0, p, 0.0)
        x_ref[r0 : r0 + PANEL, :] = done
        r1 = r0 + PANEL
        if r1 < n:
            wide = jnp.where(lane < r1, done, p)
            step = jnp.dot(p.T[r1:, :], wide, precision=HIGH, preferred_element_type=F32)
            rest = w_ref[r1:, :]
            at = lax.broadcasted_iota(jnp.int32, rest.shape, 1)
            w_ref[r1:, :] = jnp.where((at >= r0) & (at < r1), 0.0, rest) - step


def factor_front(a_ref, x_ref, w_ref):
    w_ref[...] = a_ref[...]
    factor_panels(0, 4, w_ref, x_ref)
    x_ref[4 * PANEL :, :] = w_ref[4 * PANEL :, :]


def factor_back(a_ref, x_ref, w_ref):
    w_ref[...] = a_ref[...]
    x_ref[...] = a_ref[...]
    factor_panels(4, 8, w_ref, x_ref)


def factor_half(body, x, name):
    return pl.pallas_call(
        body,
        out_shape=jax.ShapeDtypeStruct(x.shape, F32),
        scratch_shapes=[pltpu.VMEM(x.shape, F32)],
        cost_estimate=pl.CostEstimate(flops=9_000_000_000, bytes_accessed=1 << 20, transcendentals=256),
        name=name,
    )(x)


def product_kernel(flips, *refs):
    right_ref, out_ref = refs[-2:]
    order = [(z, x) for z in range(2) for x in range(2)]
    right = jnp.concatenate([right_ref[z, x] for z, x in order], axis=0)
    terms = []
    for ref, flip in zip(refs, flips):
        pieces = [ref[x, z] if flip else ref[z, x] for z, x in order]
        left = jnp.concatenate(pieces, axis=1)
        terms.append(jnp.dot(left, right, preferred_element_type=F32))
    rows = terms[0].shape[0]

    @pl.when(pl.program_id(0) == 0)
    def _():
        for i, term in enumerate(terms):
            out_ref[i * rows : (i + 1) * rows, :] = term

    @pl.when(pl.program_id(0) > 0)
    def _():
        for i, term in enumerate(terms):
            out_ref[i * rows : (i + 1) * rows, :] += term


def token_product(parts, right, name):
    width = right.shape[1]
    right = right.reshape(NZ, NX, -1, width)
    depth = right.shape[2]
    rows = parts[0][0].shape[2]

    def spot(flip, i):
        return (i % 2, i // 2, 0, 0) if flip else (i // 2, i % 2, 0, 0)

    specs = [
        pl.BlockSpec((2, 2, rows, depth), functools.partial(spot, flip)) for _, flip in parts
    ]
    specs.append(pl.BlockSpec((2, 2, depth, width), functools.partial(spot, False)))
    height = rows * len(parts)
    return pl.pallas_call(
        functools.partial(product_kernel, [flip for _, flip in parts]),
        grid=(NZ * NX // 4,),
        in_specs=specs,
        out_specs=pl.BlockSpec((height, width), lambda i: (0, 0)),
        out_shape=jax.ShapeDtypeStruct((height, width), F32),
        cost_estimate=pl.CostEstimate(
            flops=2 * height * width * DP * depth,
            bytes_accessed=2 * DP * depth * (height + width) + 4 * height * width,
            transcendentals=0,
        ),
        compiler_params=pltpu.CompilerParams(vmem_limit_bytes=24 << 20),
        name=name,
    )(*[part for part, _ in parts], right)


def contract_rows(left, right, precision=None):
    return lax.dot_general(
        left, right, (((0,), (0,)), ((), ())), precision=precision, preferred_element_type=F32
    )


def swap(x, axis):
    return lax.all_to_all(x, axis, split_axis=0, concat_axis=0, tiled=True)


def sum_scatter(x, axis, n):
    rows = x.shape[0] // n
    return jnp.sum(swap(x, axis).reshape(n, rows, x.shape[1]), axis=0)


def spread(x, axis, n):
    wide = jnp.broadcast_to(x[None], (n,) + x.shape).reshape(n * x.shape[0], x.shape[1])
    return swap(lax.optimization_barrier(wide), axis)


def shift_x(x, dx):
    pairs = [(z * NX + c, z * NX + (c + dx) % NX) for z in range(NZ) for c in range(NX)]
    return lax.ppermute(x, "dp", pairs)


def gather_z(x):
    groups = [[z * NX + c for z in range(NZ)] for c in range(NX)]
    return lax.all_gather(x, "dp", axis=0, tiled=True, axis_index_groups=groups)


def gather_tokens(x, part, coef):
    c = lax.axis_index("dp") % NX
    n = x.shape[0] // 2
    upper, lower = x[:n], x[n:]
    lower = gather_z(lower)
    line = jnp.zeros((NX,) + upper.shape, x.dtype)
    for dx in range(NX):
        piece = shift_x(upper, dx) if dx else upper
        line = lax.dynamic_update_slice(line, piece[None], ((c - dx) % NX, 0, 0))
    part, _ = lax.optimization_barrier((part, line))
    coef, _ = lax.optimization_barrier((coef, lower))
    upper = gather_z(line.reshape(NX * n, -1)).reshape(NZ, NX, n, -1)
    full = jnp.zeros((NX,) + lower.shape, x.dtype)
    half = lower.shape[0] // 2
    near, back = shift_x(lower, 1), shift_x(lower, 3)
    full = lax.dynamic_update_slice(full, lower[None], (c, 0, 0))
    full = lax.dynamic_update_slice(full, near[None], ((c - 1) % NX, 0, 0))
    full = lax.dynamic_update_slice(full, back[None], ((c + 1) % NX, 0, 0))
    far = (c + 2) % NX
    full = lax.dynamic_update_slice(full, shift_x(near[:half], 1)[None], (far, 0, 0))
    full = lax.dynamic_update_slice(full, shift_x(back[half:], 3)[None], (far, half, 0))
    return [(upper, False), (full.reshape(NX, NZ, n, -1), True)], part, coef


def shift_fs(x, dy, dc):
    pairs = [(y * 2 + c, ((y + dy) % NY) * 2 + (c + dc) % 2) for y in range(NY) for c in range(2)]
    return lax.ppermute(x, "fsdp", pairs)


def block(x, i, rows):
    return lax.dynamic_slice_in_dim(x, i * rows, rows, 0)


def fs_sum(x, kind, scale=1.0, hold=None):
    c = lax.axis_index("fsdp") % 2
    half = x.shape[0] // 2
    mine = (block(x, c, half) + shift_fs(block(x, 1 - c, half), 0, 1)).astype(kind)
    if hold is not None:
        mine, hold = lax.optimization_barrier((mine, hold))
    near, back, far = [shift_fs(mine, dy, 0).astype(F32) for dy in (1, 3, 2)]
    mine = (((mine.astype(F32) + near) + (back + far)) * scale).astype(kind)
    other = shift_fs(mine, 0, 1)
    total = jnp.concatenate([jnp.where(c == 0, mine, other), jnp.where(c == 0, other, mine)], axis=0)
    return total if hold is None else (total, hold)


def y_gather(x, cols):
    f = lax.axis_index("fsdp")
    y, c = f // 2, f % 2
    near, back = shift_fs(x, 1, 0), shift_fs(x, 3, 0)
    half = x.shape[0] // 2
    far = jnp.concatenate([shift_fs(near[:half], 1, 0), shift_fs(back[half:], 3, 0)], axis=0)
    main = jnp.zeros((DP, FS, x.shape[1], cols), x.dtype)
    rest = jnp.zeros((DP, FS, x.shape[1], x.shape[2] - cols), x.dtype)
    for part, dy in ((x, 0), (near, 1), (back, 3), (far, 2)):
        for piece, core in ((part, c), (shift_fs(part, 0, 1), 1 - c)):
            at = (0, ((y - dy) % NY) * 2 + core, 0, 0)
            main = lax.dynamic_update_slice(main, piece[:, None, :, :cols], at)
            rest = lax.dynamic_update_slice(rest, piece[:, None, :, cols:], at)
    return main.reshape(-1, cols), rest.reshape(-1, rest.shape[3])


def local(tokens, out_grad, sketch_matrix, memory):
    f = lax.axis_index("fsdp")
    cols = out_grad.shape[1] // DP
    rows = tokens.shape[0] // FS
    own = lax.dynamic_slice_in_dim(out_grad, f * rows, rows, 0)
    own = jnp.transpose(own.reshape(rows, DP, cols), (1, 0, 2))
    sk = lax.dynamic_slice_in_dim(sketch_matrix, f * rows, rows, 0)
    own = jnp.concatenate([own, jnp.broadcast_to(sk[None], (DP,) + sk.shape)], axis=2)
    own, tokens = lax.optimization_barrier((own, tokens))
    part = swap(own, "dp")
    token_part = jnp.dot(tokens, memory, preferred_element_type=F32)
    token_coef = fs_sum(token_part, BF, 1.0 / D)
    clean = jnp.transpose(tokens).astype(F32) - lax.dot_general(
        memory, token_coef, (((1,), (1,)), ((), ())), preferred_element_type=F32
    )
    clean = clean.astype(BF)
    parts, part, token_coef = gather_tokens(clean, part, token_coef)
    right, omega = y_gather(part, cols)
    mine = lax.dynamic_slice_in_dim(token_coef, f * 128, 128, 1)
    coef = contract_rows(mine, sketch_matrix)
    coef = jnp.pad(coef.reshape(DP, 4, -1), ((0, 0), (0, 4), (0, 0))).reshape(DP * 8, -1)
    coef = sum_scatter(coef, "dp", DP)
    coef = spread(coef, "dp", DP).reshape(DP, 8, -1)[:, :4].reshape(DP * 4, -1)
    coef = lax.all_gather(coef.astype(BF), "fsdp", axis=0, tiled=True)
    first = token_product(parts, omega, "first")
    gram, held = fs_sum(contract_rows(first, first, HIGH), F32, hold=right)
    half = memory.shape[0] // 2
    upper = token_product(parts[:1], right, "gradient_upper")
    lower = token_product(parts[1:], held, "gradient_lower")
    sketch = first + jnp.dot(memory, coef, preferred_element_type=F32)
    weight = contract_rows(sketch[:half], upper, lax.Precision.HIGH)
    weight = weight + contract_rows(sketch[half:], lower, lax.Precision.HIGH)
    weight = sum_scatter(weight, "fsdp", FS)
    state = factor_half(factor_front, gram, "factor_front")
    weight = spread(weight, "fsdp", FS)
    inverse = factor_half(factor_back, state, "factor_back")
    basis = lax.dot_general(first, inverse, (((1,), (1,)), ((), ())), precision=HIGH)
    coef_basis = jnp.dot(inverse, weight, precision=HIGH)
    parts = []
    for piece, side in ((upper, basis[:half]), (lower, basis[half:])):
        correction = jnp.dot(side, coef_basis, precision=lax.Precision.HIGH)
        parts.append((piece - correction).astype(BF))
    projected = jnp.concatenate(parts, axis=0)
    new_basis = (math.sqrt(D) * basis).astype(BF)
    return (projected, new_basis)


def solution(mesh):
    in_specs = (P("dp", "fsdp"), P("dp", None), P("dp", None), P("fsdp", None))
    out_specs = (P("fsdp", "dp"), P("fsdp", None))
    return jax.shard_map(local, mesh=mesh, in_specs=in_specs, out_specs=out_specs, check_vma=False)
```

```python
import math

import jax
import jax.numpy as jnp
from jax import lax
from jax.experimental import pallas as pl
from jax.experimental.pallas import tpu as pltpu
from jax.sharding import PartitionSpec as P

D = 8192
DP, FS, NY = 32, 8, 4
BF, F32 = jnp.bfloat16, jnp.float32
HIGH = lax.Precision.HIGHEST
PANEL = 32


def factor_panels(first_panel, last_panel, w_ref, x_ref):
    n = w_ref.shape[0]
    lane = lax.broadcasted_iota(jnp.int32, (PANEL, n), 1)
    sub = lax.broadcasted_iota(jnp.int32, (PANEL, n), 0)
    for r0 in range(first_panel * PANEL, last_panel * PANEL, PANEL):
        p = w_ref[r0 : r0 + PANEL, :]
        scale = jnp.ones((PANEL, n), F32)
        for j in range(0, PANEL, 2):
            c = r0 + j
            left = jnp.broadcast_to(p[:, c : c + 1], (PANEL, n))
            next_left = jnp.broadcast_to(p[:, c + 1 : c + 2], (PANEL, n))
            pivot, mixed = left[j : j + 1, :], left[j + 1 : j + 2, :]
            ratio = mixed * (1.0 / pivot)
            next_pivot = next_left[j + 1 : j + 2, :] - ratio * mixed
            at, next_at = lane == c, lane == c + 1
            row = jnp.where(at[:1], 1.0, p[j : j + 1, :])
            scaled = row * (1.0 / pivot)
            next_row = jnp.where(at[:1], 0.0, p[j + 1 : j + 2, :]) - mixed * scaled
            next_row = jnp.where(next_at[:1], 1.0, next_row)
            next_scaled = next_row * (1.0 / next_pivot)
            scaled = jnp.where(next_at[:1], 0.0, scaled)
            below = sub > j + 1
            base = jnp.where((at | next_at) & below, 0.0, p)
            base = base - jnp.where(below, left, 0.0) * scaled
            base = base - jnp.where(below, next_left - left * ratio, 0.0) * next_scaled
            p = jnp.where(sub == j, row, jnp.where(sub == j + 1, next_row, base))
            scale = jnp.where(sub == j, pivot, jnp.where(sub == j + 1, next_pivot, scale))
        p = p * lax.rsqrt(scale)
        done = jnp.where(lane <= sub + r0, p, 0.0)
        x_ref[r0 : r0 + PANEL, :] = done
        r1 = r0 + PANEL
        if r1 < n:
            wide = jnp.where(lane < r1, done, p)
            step = jnp.dot(p.T[r1:, :], wide, precision=HIGH, preferred_element_type=F32)
            rest = w_ref[r1:, :]
            at = lax.broadcasted_iota(jnp.int32, rest.shape, 1)
            w_ref[r1:, :] = jnp.where((at >= r0) & (at < r1), 0.0, rest) - step


def factor_front(a_ref, x_ref, w_ref):
    w_ref[...] = a_ref[...]
    factor_panels(0, 4, w_ref, x_ref)
    x_ref[4 * PANEL :, :] = w_ref[4 * PANEL :, :]


def factor_back(a_ref, x_ref, w_ref):
    w_ref[...] = a_ref[...]
    x_ref[...] = a_ref[...]
    factor_panels(4, 8, w_ref, x_ref)


def factor_half(body, x, name):
    return pl.pallas_call(
        body,
        out_shape=jax.ShapeDtypeStruct(x.shape, F32),
        scratch_shapes=[pltpu.VMEM(x.shape, F32)],
        cost_estimate=pl.CostEstimate(flops=9_000_000_000, bytes_accessed=1 << 20, transcendentals=256),
        name=name,
    )(x)


def contract_rows(left, right, precision=None):
    return lax.dot_general(
        left, right, (((0,), (0,)), ((), ())), precision=precision, preferred_element_type=F32
    )


def swap(x, axis):
    return lax.all_to_all(x, axis, split_axis=0, concat_axis=0, tiled=True)


def sum_scatter(x, axis, n):
    rows = x.shape[0] // n
    return jnp.sum(swap(x, axis).reshape(n, rows, x.shape[1]), axis=0)


def spread(x, axis, n):
    wide = jnp.broadcast_to(x[None], (n,) + x.shape).reshape(n * x.shape[0], x.shape[1])
    return swap(lax.optimization_barrier(wide), axis)


def shift_fs(x, dy, dc):
    pairs = [(y * 2 + c, ((y + dy) % NY) * 2 + (c + dc) % 2) for y in range(NY) for c in range(2)]
    return lax.ppermute(x, "fsdp", pairs)


def block(x, i, rows):
    return lax.dynamic_slice_in_dim(x, i * rows, rows, 0)


def fs_sum(x, kind, scale=1.0, hold=None):
    c = lax.axis_index("fsdp") % 2
    half = x.shape[0] // 2
    mine = (block(x, c, half) + shift_fs(block(x, 1 - c, half), 0, 1)).astype(kind)
    if hold is not None:
        mine, hold = lax.optimization_barrier((mine, hold))
    near, back, far = [shift_fs(mine, dy, 0).astype(F32) for dy in (1, 3, 2)]
    mine = (((mine.astype(F32) + near) + (back + far)) * scale).astype(kind)
    other = shift_fs(mine, 0, 1)
    total = jnp.concatenate([jnp.where(c == 0, mine, other), jnp.where(c == 0, other, mine)], axis=0)
    return total if hold is None else (total, hold)


def y_gather(x, cols, other):
    f = lax.axis_index("fsdp")
    y, c = f // 2, f % 2
    main = jnp.zeros((DP, FS, x.shape[1], cols), x.dtype)
    rest = jnp.zeros((DP, FS, x.shape[1], x.shape[2] - cols), x.dtype)

    def put(full, part, dy):
        main, rest = full
        for piece, core in ((part, c), (shift_fs(part, 0, 1), 1 - c)):
            at = (0, ((y - dy) % NY) * 2 + core, 0, 0)
            main = lax.dynamic_update_slice(main, piece[:, None, :, :cols], at)
            rest = lax.dynamic_update_slice(rest, piece[:, None, :, cols:], at)
        return main, rest

    near, back = shift_fs(x, 1, 0), shift_fs(x, 3, 0)
    full = put((main, rest), x, 0)
    half = x.shape[0] // 2
    far = jnp.concatenate([shift_fs(near[:half], 1, 0), shift_fs(back[half:], 3, 0)], axis=0)
    full = put(put(full, near, 1), back, 3)
    far, full, other = lax.optimization_barrier((far, full, other))
    main, rest = put(full, far, 2)
    return main.reshape(-1, cols), rest.reshape(-1, rest.shape[3]), other


def local(tokens, out_grad, sketch_matrix, memory):
    f = lax.axis_index("fsdp")
    cols = out_grad.shape[1] // DP
    rows = tokens.shape[0] // FS
    own = lax.dynamic_slice_in_dim(out_grad, f * rows, rows, 0)
    own = jnp.transpose(own.reshape(rows, DP, cols), (1, 0, 2))
    sk = lax.dynamic_slice_in_dim(sketch_matrix, f * rows, rows, 0)
    own = jnp.concatenate([own, jnp.broadcast_to(sk[None], (DP,) + sk.shape)], axis=2)
    part = swap(own, "dp")
    token_part = jnp.dot(tokens, memory, preferred_element_type=F32)
    token_coef = fs_sum(token_part, BF, 1.0 / D)
    clean = tokens.astype(F32) - lax.dot_general(
        token_coef, memory, (((1,), (1,)), ((), ())), preferred_element_type=F32
    )
    clean = clean.astype(BF)
    clean_all = lax.all_gather(clean, "dp", axis=0, tiled=True)
    part, clean, token_coef = lax.optimization_barrier((part, clean, token_coef))
    mine = lax.dynamic_slice_in_dim(token_coef, f * 128, 128, 1)
    coef = contract_rows(mine, sketch_matrix)
    coef = jnp.pad(coef.reshape(DP, 4, -1), ((0, 0), (0, 4), (0, 0))).reshape(DP * 8, -1)
    coef = sum_scatter(coef, "dp", DP)
    coef = spread(coef, "dp", DP).reshape(DP, 8, -1)[:, :4].reshape(DP * 4, -1)
    coef = lax.all_gather(coef.astype(BF), "fsdp", axis=0, tiled=True)
    right, omega, coef = y_gather(part, cols, coef)
    first = contract_rows(clean_all, omega)
    gram, held = fs_sum(contract_rows(first, first, HIGH), F32, hold=clean_all)
    half = memory.shape[0] // 2
    upper = contract_rows(clean_all[:, :half], right)
    lower = contract_rows(held[:, half:], right)
    sketch = first + jnp.dot(memory, coef, preferred_element_type=F32)
    weight = contract_rows(sketch[:half], upper, lax.Precision.HIGH)
    weight = weight + contract_rows(sketch[half:], lower, lax.Precision.HIGH)
    weight = sum_scatter(weight, "fsdp", FS)
    state = factor_half(factor_front, gram, "factor_front")
    weight = spread(weight, "fsdp", FS)
    inverse = factor_half(factor_back, state, "factor_back")
    basis = lax.dot_general(first, inverse, (((1,), (1,)), ((), ())), precision=HIGH)
    coef_basis = jnp.dot(inverse, weight, precision=HIGH)
    parts = []
    for piece, side in ((upper, basis[:half]), (lower, basis[half:])):
        correction = jnp.dot(side, coef_basis, precision=lax.Precision.HIGH)
        parts.append((piece - correction).astype(BF))
    projected = jnp.concatenate(parts, axis=0)
    new_basis = (math.sqrt(D) * basis).astype(BF)
    return (projected, new_basis)


def solution(mesh):
    in_specs = (P("dp", "fsdp"), P("dp", None), P("dp", None), P("fsdp", None))
    out_specs = (P("fsdp", "dp"), P("fsdp", None))
    return jax.shard_map(local, mesh=mesh, in_specs=in_specs, out_specs=out_specs, check_vma=False)
```

```python
import math

import jax
import jax.numpy as jnp
from jax import lax
from jax.experimental import pallas as pl
from jax.experimental.pallas import tpu as pltpu
from jax.sharding import PartitionSpec as P

D = 8192
DP, FS, NY = 32, 8, 4
BF, F32 = jnp.bfloat16, jnp.float32
HIGH = lax.Precision.HIGHEST
PANEL = 32


def factor_panels(first_panel, last_panel, w_ref, x_ref):
    n = w_ref.shape[0]
    lane = lax.broadcasted_iota(jnp.int32, (PANEL, n), 1)
    sub = lax.broadcasted_iota(jnp.int32, (PANEL, n), 0)
    for r0 in range(first_panel * PANEL, last_panel * PANEL, PANEL):
        p = w_ref[r0 : r0 + PANEL, :]
        scale = jnp.ones((PANEL, n), F32)
        for j in range(0, PANEL, 2):
            c = r0 + j
            left = jnp.broadcast_to(p[:, c : c + 1], (PANEL, n))
            next_left = jnp.broadcast_to(p[:, c + 1 : c + 2], (PANEL, n))
            pivot, mixed = left[j : j + 1, :], left[j + 1 : j + 2, :]
            ratio = mixed * (1.0 / pivot)
            next_pivot = next_left[j + 1 : j + 2, :] - ratio * mixed
            at, next_at = lane == c, lane == c + 1
            row = jnp.where(at[:1], 1.0, p[j : j + 1, :])
            scaled = row * (1.0 / pivot)
            next_row = jnp.where(at[:1], 0.0, p[j + 1 : j + 2, :]) - mixed * scaled
            next_row = jnp.where(next_at[:1], 1.0, next_row)
            next_scaled = next_row * (1.0 / next_pivot)
            scaled = jnp.where(next_at[:1], 0.0, scaled)
            below = sub > j + 1
            base = jnp.where((at | next_at) & below, 0.0, p)
            base = base - jnp.where(below, left, 0.0) * scaled
            base = base - jnp.where(below, next_left - left * ratio, 0.0) * next_scaled
            p = jnp.where(sub == j, row, jnp.where(sub == j + 1, next_row, base))
            scale = jnp.where(sub == j, pivot, jnp.where(sub == j + 1, next_pivot, scale))
        p = p * lax.rsqrt(scale)
        done = jnp.where(lane <= sub + r0, p, 0.0)
        x_ref[r0 : r0 + PANEL, :] = done
        r1 = r0 + PANEL
        if r1 < n:
            wide = jnp.where(lane < r1, done, p)
            step = jnp.dot(p.T[r1:, :], wide, precision=HIGH, preferred_element_type=F32)
            rest = w_ref[r1:, :]
            at = lax.broadcasted_iota(jnp.int32, rest.shape, 1)
            w_ref[r1:, :] = jnp.where((at >= r0) & (at < r1), 0.0, rest) - step


def factor_front(a_ref, x_ref, w_ref):
    w_ref[...] = a_ref[...]
    factor_panels(0, 4, w_ref, x_ref)
    x_ref[4 * PANEL :, :] = w_ref[4 * PANEL :, :]


def factor_back(a_ref, x_ref, w_ref):
    w_ref[...] = a_ref[...]
    x_ref[...] = a_ref[...]
    factor_panels(4, 8, w_ref, x_ref)


def factor_half(body, x, name):
    return pl.pallas_call(
        body,
        out_shape=jax.ShapeDtypeStruct(x.shape, F32),
        scratch_shapes=[pltpu.VMEM(x.shape, F32)],
        cost_estimate=pl.CostEstimate(flops=9_000_000_000, bytes_accessed=1 << 20, transcendentals=256),
        name=name,
    )(x)


def contract_rows(left, right, precision=None):
    return lax.dot_general(
        left, right, (((0,), (0,)), ((), ())), precision=precision, preferred_element_type=F32
    )


def swap(x, axis):
    return lax.all_to_all(x, axis, split_axis=0, concat_axis=0, tiled=True)


def sum_scatter(x, axis, n):
    rows = x.shape[0] // n
    return jnp.sum(swap(x, axis).reshape(n, rows, x.shape[1]), axis=0)


def spread(x, axis, n):
    wide = jnp.broadcast_to(x[None], (n,) + x.shape).reshape(n * x.shape[0], x.shape[1])
    return swap(lax.optimization_barrier(wide), axis)


def shift_fs(x, dy, dc):
    pairs = [(y * 2 + c, ((y + dy) % NY) * 2 + (c + dc) % 2) for y in range(NY) for c in range(2)]
    return lax.ppermute(x, "fsdp", pairs)


def block(x, i, rows):
    return lax.dynamic_slice_in_dim(x, i * rows, rows, 0)


def fs_sum(x, kind, scale=1.0, hold=None):
    c = lax.axis_index("fsdp") % 2
    half = x.shape[0] // 2
    mine = (block(x, c, half) + shift_fs(block(x, 1 - c, half), 0, 1)).astype(kind)
    if hold is not None:
        mine, hold = lax.optimization_barrier((mine, hold))
    near, back, far = [shift_fs(mine, dy, 0).astype(F32) for dy in (1, 3, 2)]
    mine = (((mine.astype(F32) + near) + (back + far)) * scale).astype(kind)
    other = shift_fs(mine, 0, 1)
    total = jnp.concatenate([jnp.where(c == 0, mine, other), jnp.where(c == 0, other, mine)], axis=0)
    return total if hold is None else (total, hold)


def fs_gather(x):
    f = lax.axis_index("fsdp")
    y, c = f // 2, f % 2
    line = jnp.zeros((NY,) + x.shape, x.dtype)
    for dy in range(NY):
        piece = shift_fs(x, dy, 0) if dy else x
        line = lax.dynamic_update_slice(line, piece[None], ((y - dy) % NY, 0, 0))
    other = shift_fs(line, 0, 1)
    pair = jnp.stack([jnp.where(c == 0, line, other), jnp.where(c == 0, other, line)], axis=1)
    return pair.reshape(FS * x.shape[0], x.shape[1])


def y_gather(x, cols, other):
    f = lax.axis_index("fsdp")
    y, c = f // 2, f % 2
    main = jnp.zeros((DP, FS, x.shape[1], cols), x.dtype)
    rest = jnp.zeros((DP, FS, x.shape[1], x.shape[2] - cols), x.dtype)

    def put(full, part, dy):
        main, rest = full
        for piece, core in ((part, c), (shift_fs(part, 0, 1), 1 - c)):
            at = (0, ((y - dy) % NY) * 2 + core, 0, 0)
            main = lax.dynamic_update_slice(main, piece[:, None, :, :cols], at)
            rest = lax.dynamic_update_slice(rest, piece[:, None, :, cols:], at)
        return main, rest

    near, back = shift_fs(x, 1, 0), shift_fs(x, 3, 0)
    full = put((main, rest), x, 0)
    half = x.shape[0] // 2
    far = jnp.concatenate([shift_fs(near[:half], 1, 0), shift_fs(back[half:], 3, 0)], axis=0)
    full = put(put(full, near, 1), back, 3)
    far, full, other = lax.optimization_barrier((far, full, other))
    main, rest = put(full, far, 2)
    return main.reshape(-1, cols), rest.reshape(-1, rest.shape[3]), other


def local(tokens, out_grad, sketch_matrix, memory):
    f = lax.axis_index("fsdp")
    cols = out_grad.shape[1] // DP
    rows = tokens.shape[0] // FS
    own = lax.dynamic_slice_in_dim(out_grad, f * rows, rows, 0)
    own = jnp.transpose(own.reshape(rows, DP, cols), (1, 0, 2))
    sk = lax.dynamic_slice_in_dim(sketch_matrix, f * rows, rows, 0)
    own = jnp.concatenate([own, jnp.broadcast_to(sk[None], (DP,) + sk.shape)], axis=2)
    part = swap(own, "dp")
    token_part = jnp.dot(tokens, memory, preferred_element_type=F32)
    token_coef = fs_sum(token_part, BF, 1.0 / D)
    clean = tokens.astype(F32) - lax.dot_general(
        token_coef, memory, (((1,), (1,)), ((), ())), preferred_element_type=F32
    )
    clean = clean.astype(BF)
    clean_all = lax.all_gather(clean, "dp", axis=0, tiled=True)
    part, clean, token_coef = lax.optimization_barrier((part, clean, token_coef))
    mine = lax.dynamic_slice_in_dim(token_coef, f * 128, 128, 1)
    coef = contract_rows(mine, sketch_matrix)
    coef = jnp.pad(coef.reshape(DP, 4, -1), ((0, 0), (0, 4), (0, 0))).reshape(DP * 8, -1)
    coef = sum_scatter(coef, "dp", DP)
    coef = spread(coef, "dp", DP).reshape(DP, 8, -1)[:, :4].reshape(DP * 4, -1)
    right, omega, coef = y_gather(part, cols, coef.astype(BF))
    coef = fs_gather(coef)
    first = contract_rows(clean_all, omega)
    gram, held = fs_sum(contract_rows(first, first, HIGH), F32, hold=clean_all)
    half = memory.shape[0] // 2
    upper = contract_rows(clean_all[:, :half], right)
    lower = contract_rows(held[:, half:], right)
    sketch = first + jnp.dot(memory, coef, preferred_element_type=F32)
    weight = contract_rows(sketch[:half], upper, lax.Precision.HIGH)
    weight = weight + contract_rows(sketch[half:], lower, lax.Precision.HIGH)
    weight = sum_scatter(weight, "fsdp", FS)
    state = factor_half(factor_front, gram, "factor_front")
    weight = spread(weight, "fsdp", FS)
    inverse = factor_half(factor_back, state, "factor_back")
    basis = lax.dot_general(first, inverse, (((1,), (1,)), ((), ())), precision=lax.Precision.HIGH)
    coef_basis = jnp.dot(inverse, weight, precision=lax.Precision.HIGH)
    parts = []
    for piece, side in ((upper, basis[:half]), (lower, basis[half:])):
        correction = jnp.dot(side, coef_basis, precision=lax.Precision.HIGH)
        parts.append((piece - correction).astype(BF))
    projected = jnp.concatenate(parts, axis=0)
    new_basis = (math.sqrt(D) * basis).astype(BF)
    return (projected, new_basis)


def solution(mesh):
    in_specs = (P("dp", "fsdp"), P("dp", None), P("dp", None), P("fsdp", None))
    out_specs = (P("fsdp", "dp"), P("fsdp", None))
    return jax.shard_map(local, mesh=mesh, in_specs=in_specs, out_specs=out_specs, check_vma=False)
```

```python
import math

import jax
import jax.numpy as jnp
from jax import lax
from jax.experimental import pallas as pl
from jax.experimental.pallas import tpu as pltpu
from jax.sharding import PartitionSpec as P

D = 8192
DP, FS, NY = 32, 8, 4
BF, F32 = jnp.bfloat16, jnp.float32
HIGH = lax.Precision.HIGHEST
PANEL = 32


def factor_panels(first_panel, last_panel, w_ref, x_ref):
    n = w_ref.shape[0]
    lane = lax.broadcasted_iota(jnp.int32, (PANEL, n), 1)
    sub = lax.broadcasted_iota(jnp.int32, (PANEL, n), 0)
    for r0 in range(first_panel * PANEL, last_panel * PANEL, PANEL):
        p = w_ref[r0 : r0 + PANEL, :]
        scale = jnp.ones((PANEL, n), F32)
        for j in range(0, PANEL, 2):
            c = r0 + j
            left = jnp.broadcast_to(p[:, c : c + 1], (PANEL, n))
            next_left = jnp.broadcast_to(p[:, c + 1 : c + 2], (PANEL, n))
            pivot, mixed = left[j : j + 1, :], left[j + 1 : j + 2, :]
            ratio = mixed * (1.0 / pivot)
            next_pivot = next_left[j + 1 : j + 2, :] - ratio * mixed
            at, next_at = lane == c, lane == c + 1
            row = jnp.where(at[:1], 1.0, p[j : j + 1, :])
            scaled = row * (1.0 / pivot)
            next_row = jnp.where(at[:1], 0.0, p[j + 1 : j + 2, :]) - mixed * scaled
            next_row = jnp.where(next_at[:1], 1.0, next_row)
            next_scaled = next_row * (1.0 / next_pivot)
            scaled = jnp.where(next_at[:1], 0.0, scaled)
            below = sub > j + 1
            base = jnp.where((at | next_at) & below, 0.0, p)
            base = base - jnp.where(below, left, 0.0) * scaled
            base = base - jnp.where(below, next_left - left * ratio, 0.0) * next_scaled
            p = jnp.where(sub == j, row, jnp.where(sub == j + 1, next_row, base))
            scale = jnp.where(sub == j, pivot, jnp.where(sub == j + 1, next_pivot, scale))
        p = p * lax.rsqrt(scale)
        done = jnp.where(lane <= sub + r0, p, 0.0)
        x_ref[r0 : r0 + PANEL, :] = done
        r1 = r0 + PANEL
        if r1 < n:
            wide = jnp.where(lane < r1, done, p)
            step = jnp.dot(p.T[r1:, :], wide, precision=HIGH, preferred_element_type=F32)
            rest = w_ref[r1:, :]
            at = lax.broadcasted_iota(jnp.int32, rest.shape, 1)
            w_ref[r1:, :] = jnp.where((at >= r0) & (at < r1), 0.0, rest) - step


def factor_front(a_ref, x_ref, w_ref):
    w_ref[...] = a_ref[...]
    factor_panels(0, 4, w_ref, x_ref)
    x_ref[4 * PANEL :, :] = w_ref[4 * PANEL :, :]


def factor_back(a_ref, x_ref, w_ref):
    w_ref[...] = a_ref[...]
    x_ref[...] = a_ref[...]
    factor_panels(4, 8, w_ref, x_ref)


def factor_half(body, x, name):
    return pl.pallas_call(
        body,
        out_shape=jax.ShapeDtypeStruct(x.shape, F32),
        scratch_shapes=[pltpu.VMEM(x.shape, F32)],
        cost_estimate=pl.CostEstimate(flops=9_000_000_000, bytes_accessed=1 << 20, transcendentals=256),
        name=name,
    )(x)


def contract_rows(left, right, precision=None):
    return lax.dot_general(
        left, right, (((0,), (0,)), ((), ())), precision=precision, preferred_element_type=F32
    )


def swap(x, axis):
    return lax.all_to_all(x, axis, split_axis=0, concat_axis=0, tiled=True)


def sum_scatter(x, axis, n):
    rows = x.shape[0] // n
    return jnp.sum(swap(x, axis).reshape(n, rows, x.shape[1]), axis=0)


def spread(x, axis, n):
    wide = jnp.broadcast_to(x[None], (n,) + x.shape).reshape(n * x.shape[0], x.shape[1])
    return swap(lax.optimization_barrier(wide), axis)


def shift_fs(x, dy, dc):
    pairs = [(y * 2 + c, ((y + dy) % NY) * 2 + (c + dc) % 2) for y in range(NY) for c in range(2)]
    return lax.ppermute(x, "fsdp", pairs)


def block(x, i, rows):
    return lax.dynamic_slice_in_dim(x, i * rows, rows, 0)


def fs_sum(x, kind, scale=1.0, hold=None):
    c = lax.axis_index("fsdp") % 2
    half = x.shape[0] // 2
    mine = (block(x, c, half) + shift_fs(block(x, 1 - c, half), 0, 1)).astype(kind)
    if hold is not None:
        mine, hold = lax.optimization_barrier((mine, hold))
    near, back, far = [shift_fs(mine, dy, 0).astype(F32) for dy in (1, 3, 2)]
    mine = (((mine.astype(F32) + near) + (back + far)) * scale).astype(kind)
    other = shift_fs(mine, 0, 1)
    total = jnp.concatenate([jnp.where(c == 0, mine, other), jnp.where(c == 0, other, mine)], axis=0)
    return total if hold is None else (total, hold)


def fs_gather(x):
    f = lax.axis_index("fsdp")
    y, c = f // 2, f % 2
    line = jnp.zeros((NY,) + x.shape, x.dtype)
    for dy in range(NY):
        piece = shift_fs(x, dy, 0) if dy else x
        line = lax.dynamic_update_slice(line, piece[None], ((y - dy) % NY, 0, 0))
    other = shift_fs(line, 0, 1)
    pair = jnp.stack([jnp.where(c == 0, line, other), jnp.where(c == 0, other, line)], axis=1)
    return pair.reshape(FS * x.shape[0], x.shape[1])


def y_gather(x, cols, other):
    f = lax.axis_index("fsdp")
    y, c = f // 2, f % 2
    main = jnp.zeros((DP, FS, x.shape[1], cols), x.dtype)
    rest = jnp.zeros((DP, FS, x.shape[1], x.shape[2] - cols), x.dtype)

    def put(full, part, dy):
        main, rest = full
        for piece, core in ((part, c), (shift_fs(part, 0, 1), 1 - c)):
            at = (0, ((y - dy) % NY) * 2 + core, 0, 0)
            main = lax.dynamic_update_slice(main, piece[:, None, :, :cols], at)
            rest = lax.dynamic_update_slice(rest, piece[:, None, :, cols:], at)
        return main, rest

    near, back = shift_fs(x, 1, 0), shift_fs(x, 3, 0)
    full = put((main, rest), x, 0)
    half = x.shape[0] // 2
    far = jnp.concatenate([shift_fs(near[:half], 1, 0), shift_fs(back[half:], 3, 0)], axis=0)
    far, full, other = lax.optimization_barrier((far, full, other))
    main, rest = put(put(put(full, near, 1), back, 3), far, 2)
    return main.reshape(-1, cols), rest.reshape(-1, rest.shape[3]), other


def local(tokens, out_grad, sketch_matrix, memory):
    f = lax.axis_index("fsdp")
    cols = out_grad.shape[1] // DP
    rows = tokens.shape[0] // FS
    own = lax.dynamic_slice_in_dim(out_grad, f * rows, rows, 0)
    own = jnp.transpose(own.reshape(rows, DP, cols), (1, 0, 2))
    sk = lax.dynamic_slice_in_dim(sketch_matrix, f * rows, rows, 0)
    own = jnp.concatenate([own, jnp.broadcast_to(sk[None], (DP,) + sk.shape)], axis=2)
    part = swap(own, "dp")
    token_part = jnp.dot(tokens, memory, preferred_element_type=F32)
    token_coef = fs_sum(token_part, BF, 1.0 / D)
    clean = tokens.astype(F32) - lax.dot_general(
        token_coef, memory, (((1,), (1,)), ((), ())), preferred_element_type=F32
    )
    clean = clean.astype(BF)
    clean_all = lax.all_gather(clean, "dp", axis=0, tiled=True)
    part, clean, token_coef = lax.optimization_barrier((part, clean, token_coef))
    mine = lax.dynamic_slice_in_dim(token_coef, f * 128, 128, 1)
    coef = contract_rows(mine, sketch_matrix)
    coef = jnp.pad(coef.reshape(DP, 4, -1), ((0, 0), (0, 4), (0, 0))).reshape(DP * 8, -1)
    coef = sum_scatter(coef, "dp", DP)
    coef = spread(coef, "dp", DP).reshape(DP, 8, -1)[:, :4].reshape(DP * 4, -1)
    right, omega, coef = y_gather(part, cols, coef.astype(BF))
    coef = fs_gather(coef)
    first = contract_rows(clean_all, omega)
    gram, held = fs_sum(contract_rows(first, first, HIGH), F32, hold=clean_all)
    half = memory.shape[0] // 2
    gradient = contract_rows(held, right)
    sketch = first + jnp.dot(memory, coef, preferred_element_type=F32)
    weight = contract_rows(sketch, gradient, lax.Precision.HIGH)
    weight = sum_scatter(weight, "fsdp", FS)
    state = factor_half(factor_front, gram, "factor_front")
    weight = spread(weight, "fsdp", FS)
    inverse = factor_half(factor_back, state, "factor_back")
    basis = lax.dot_general(first, inverse, (((1,), (1,)), ((), ())), precision=lax.Precision.HIGH)
    coef_basis = jnp.dot(inverse, weight, precision=lax.Precision.HIGH)
    parts = []
    for piece, side in ((gradient[:half], basis[:half]), (gradient[half:], basis[half:])):
        correction = jnp.dot(side, coef_basis, precision=lax.Precision.HIGH)
        parts.append((piece - correction).astype(BF))
    projected = jnp.concatenate(parts, axis=0)
    new_basis = (math.sqrt(D) * basis).astype(BF)
    return (projected, new_basis)


def solution(mesh):
    in_specs = (P("dp", "fsdp"), P("dp", None), P("dp", None), P("fsdp", None))
    out_specs = (P("fsdp", "dp"), P("fsdp", None))
    return jax.shard_map(local, mesh=mesh, in_specs=in_specs, out_specs=out_specs, check_vma=False)
```

```python
import math

import jax
import jax.numpy as jnp
from jax import lax
from jax.experimental import pallas as pl
from jax.experimental.pallas import tpu as pltpu
from jax.sharding import PartitionSpec as P

D = 8192
DP, FS, NY = 32, 8, 4
BF, F32 = jnp.bfloat16, jnp.float32
HIGH = lax.Precision.HIGHEST
PANEL = 32


def factor_panels(first_panel, last_panel, w_ref, x_ref):
    n = w_ref.shape[0]
    lane = lax.broadcasted_iota(jnp.int32, (PANEL, n), 1)
    sub = lax.broadcasted_iota(jnp.int32, (PANEL, n), 0)
    for r0 in range(first_panel * PANEL, last_panel * PANEL, PANEL):
        p = w_ref[r0 : r0 + PANEL, :]
        scale = jnp.ones((PANEL, n), F32)
        for j in range(0, PANEL, 2):
            c = r0 + j
            left = jnp.broadcast_to(p[:, c : c + 1], (PANEL, n))
            next_left = jnp.broadcast_to(p[:, c + 1 : c + 2], (PANEL, n))
            pivot, mixed = left[j : j + 1, :], left[j + 1 : j + 2, :]
            ratio = mixed * (1.0 / pivot)
            next_pivot = next_left[j + 1 : j + 2, :] - ratio * mixed
            at, next_at = lane == c, lane == c + 1
            row = jnp.where(at[:1], 1.0, p[j : j + 1, :])
            scaled = row * (1.0 / pivot)
            next_row = jnp.where(at[:1], 0.0, p[j + 1 : j + 2, :]) - mixed * scaled
            next_row = jnp.where(next_at[:1], 1.0, next_row)
            next_scaled = next_row * (1.0 / next_pivot)
            scaled = jnp.where(next_at[:1], 0.0, scaled)
            below = sub > j + 1
            base = jnp.where((at | next_at) & below, 0.0, p)
            base = base - jnp.where(below, left, 0.0) * scaled
            base = base - jnp.where(below, next_left - left * ratio, 0.0) * next_scaled
            p = jnp.where(sub == j, row, jnp.where(sub == j + 1, next_row, base))
            scale = jnp.where(sub == j, pivot, jnp.where(sub == j + 1, next_pivot, scale))
        p = p * lax.rsqrt(scale)
        done = jnp.where(lane <= sub + r0, p, 0.0)
        x_ref[r0 : r0 + PANEL, :] = done
        r1 = r0 + PANEL
        if r1 < n:
            wide = jnp.where(lane < r1, done, p)
            step = jnp.dot(p.T[r1:, :], wide, precision=HIGH, preferred_element_type=F32)
            rest = w_ref[r1:, :]
            at = lax.broadcasted_iota(jnp.int32, rest.shape, 1)
            w_ref[r1:, :] = jnp.where((at >= r0) & (at < r1), 0.0, rest) - step


def factor_front(a_ref, x_ref, w_ref):
    w_ref[...] = a_ref[...]
    factor_panels(0, 4, w_ref, x_ref)
    x_ref[4 * PANEL :, :] = w_ref[4 * PANEL :, :]


def factor_back(a_ref, x_ref, w_ref):
    w_ref[...] = a_ref[...]
    x_ref[...] = a_ref[...]
    factor_panels(4, 8, w_ref, x_ref)


def factor_half(body, x, name):
    return pl.pallas_call(
        body,
        out_shape=jax.ShapeDtypeStruct(x.shape, F32),
        scratch_shapes=[pltpu.VMEM(x.shape, F32)],
        cost_estimate=pl.CostEstimate(flops=9_000_000_000, bytes_accessed=1 << 20, transcendentals=256),
        name=name,
    )(x)


def contract_rows(left, right, precision=None):
    return lax.dot_general(
        left, right, (((0,), (0,)), ((), ())), precision=precision, preferred_element_type=F32
    )


def swap(x, axis):
    return lax.all_to_all(x, axis, split_axis=0, concat_axis=0, tiled=True)


def sum_scatter(x, axis, n):
    rows = x.shape[0] // n
    return jnp.sum(swap(x, axis).reshape(n, rows, x.shape[1]), axis=0)


def spread(x, axis, n):
    wide = jnp.broadcast_to(x[None], (n,) + x.shape).reshape(n * x.shape[0], x.shape[1])
    return swap(lax.optimization_barrier(wide), axis)


def shift_fs(x, dy, dc):
    pairs = [(y * 2 + c, ((y + dy) % NY) * 2 + (c + dc) % 2) for y in range(NY) for c in range(2)]
    return lax.ppermute(x, "fsdp", pairs)


def block(x, i, rows):
    return lax.dynamic_slice_in_dim(x, i * rows, rows, 0)


def fs_sum(x, kind, scale=1.0, hold=None):
    c = lax.axis_index("fsdp") % 2
    half = x.shape[0] // 2
    mine = (block(x, c, half) + shift_fs(block(x, 1 - c, half), 0, 1)).astype(kind)
    if hold is not None:
        mine, hold = lax.optimization_barrier((mine, hold))
    near, back, far = [shift_fs(mine, dy, 0).astype(F32) for dy in (1, 3, 2)]
    mine = (((mine.astype(F32) + near) + (back + far)) * scale).astype(kind)
    other = shift_fs(mine, 0, 1)
    total = jnp.concatenate([jnp.where(c == 0, mine, other), jnp.where(c == 0, other, mine)], axis=0)
    return total if hold is None else (total, hold)


def fs_gather(x):
    f = lax.axis_index("fsdp")
    y, c = f // 2, f % 2
    line = jnp.zeros((NY,) + x.shape, x.dtype)
    for dy in range(NY):
        piece = shift_fs(x, dy, 0) if dy else x
        line = lax.dynamic_update_slice(line, piece[None], ((y - dy) % NY, 0, 0))
    other = shift_fs(line, 0, 1)
    pair = jnp.stack([jnp.where(c == 0, line, other), jnp.where(c == 0, other, line)], axis=1)
    return pair.reshape(FS * x.shape[0], x.shape[1])


def y_gather(x, cols, other):
    f = lax.axis_index("fsdp")
    y, c = f // 2, f % 2
    full = jnp.zeros((DP, FS) + x.shape[1:], x.dtype)

    def put(full, part, dy):
        for piece, core in ((part, c), (shift_fs(part, 0, 1), 1 - c)):
            at = (0, ((y - dy) % NY) * 2 + core, 0, 0)
            full = lax.dynamic_update_slice(full, piece[:, None], at)
        return full

    near, back = shift_fs(x, 1, 0), shift_fs(x, 3, 0)
    full = put(full, x, 0)
    half = x.shape[0] // 2
    far = jnp.concatenate([shift_fs(near[:half], 1, 0), shift_fs(back[half:], 3, 0)], axis=0)
    full = put(put(full, near, 1), back, 3)
    far, full, other = lax.optimization_barrier((far, full, other))
    full = put(full, far, 2).reshape(-1, x.shape[2])
    return full[:, :cols], full[:, cols:], other


def local(tokens, out_grad, sketch_matrix, memory):
    f = lax.axis_index("fsdp")
    cols = out_grad.shape[1] // DP
    rows = tokens.shape[0] // FS
    own = lax.dynamic_slice_in_dim(out_grad, f * rows, rows, 0)
    own = jnp.transpose(own.reshape(rows, DP, cols), (1, 0, 2))
    sk = lax.dynamic_slice_in_dim(sketch_matrix, f * rows, rows, 0)
    own = jnp.concatenate([own, jnp.broadcast_to(sk[None], (DP,) + sk.shape)], axis=2)
    part = swap(own, "dp")
    token_part = jnp.dot(tokens, memory, preferred_element_type=F32)
    token_coef = fs_sum(token_part, BF, 1.0 / D)
    clean = tokens.astype(F32) - lax.dot_general(
        token_coef, memory, (((1,), (1,)), ((), ())), preferred_element_type=F32
    )
    clean = clean.astype(BF)
    clean_all = lax.all_gather(clean, "dp", axis=0, tiled=True)
    part, clean, token_coef = lax.optimization_barrier((part, clean, token_coef))
    mine = lax.dynamic_slice_in_dim(token_coef, f * 128, 128, 1)
    coef = contract_rows(mine, sketch_matrix)
    coef = jnp.pad(coef.reshape(DP, 4, -1), ((0, 0), (0, 4), (0, 0))).reshape(DP * 8, -1)
    coef = sum_scatter(coef, "dp", DP)
    coef = spread(coef, "dp", DP).reshape(DP, 8, -1)[:, :4].reshape(DP * 4, -1)
    right, omega, coef = y_gather(part, cols, coef.astype(BF))
    coef = fs_gather(coef)
    first = contract_rows(clean_all, omega)
    gram, held = fs_sum(contract_rows(first, first, HIGH), F32, hold=clean_all)
    half = memory.shape[0] // 2
    upper = contract_rows(clean_all[:, :half], right)
    lower = contract_rows(held[:, half:], right)
    sketch = first + jnp.dot(memory, coef, preferred_element_type=F32)
    weight = contract_rows(sketch[:half], upper, lax.Precision.HIGH)
    weight = weight + contract_rows(sketch[half:], lower, lax.Precision.HIGH)
    weight = sum_scatter(weight, "fsdp", FS)
    state = factor_half(factor_front, gram, "factor_front")
    weight = spread(weight, "fsdp", FS)
    inverse = factor_half(factor_back, state, "factor_back")
    basis = lax.dot_general(first, inverse, (((1,), (1,)), ((), ())), precision=lax.Precision.HIGH)
    coef_basis = jnp.dot(inverse, weight, precision=lax.Precision.HIGH)
    parts = []
    for piece, side in ((upper, basis[:half]), (lower, basis[half:])):
        correction = jnp.dot(side, coef_basis, precision=lax.Precision.HIGH)
        parts.append((piece - correction).astype(BF))
    projected = jnp.concatenate(parts, axis=0)
    new_basis = (math.sqrt(D) * basis).astype(BF)
    return (projected, new_basis)


def solution(mesh):
    in_specs = (P("dp", "fsdp"), P("dp", None), P("dp", None), P("fsdp", None))
    out_specs = (P("fsdp", "dp"), P("fsdp", None))
    return jax.shard_map(local, mesh=mesh, in_specs=in_specs, out_specs=out_specs, check_vma=False)
```
